512 devices in a mesh: frame: 64 (over z, x_lo, core), row: 8 (over y, x_hi).
Axes of the slice: x: 4 (x_hi: 2, x_lo: 2; x = x_hi * 2 + x_lo), y: 4, z: 16, core: 2. Of those that a mesh axis runs over, the one named last changes fastest.
Arguments:
- video: bfloat16 [64, 32, 32, 3072], P('frame', 'row'), may hold values from -18 to 18
- qkv_weight: bfloat16 [3072, 3, 2048], P('frame', None, 'row'), may hold values from -1 to 1
- window: int32 [16, 3], P('row'), may hold values from 0 to 1, as said below
- clips: int32 [64], replicated, may hold values from 0 to 15, never falling along the last dimension, each value on 1 to 8 neighbouring positions
Outputs:
- attended: bfloat16 [64, 32, 32, 2048], P('frame', None, None, 'row')
The draws below stay inside these ranges and needn't reach their ends.
Inputs may be any that keep to these rules, and one draw needn't show every extreme that they name: window[h, 0], window[h, 1] and window[h, 2] are head h's reaches along frames, row tiles and column tiles; in every group of 2 consecutive heads along each of the three, some head has reach 1. `clips`: clip numbers never fall along the frames; each clip has 1 to 8 frames.
All inputs are finite; a program needn't handle non-finite values.
Results may differ from the reference program's by a relative error of at most 0.0068.
Values may be sent and summed in bfloat16 or wider, within the bound.
No kernel may reach another device: no remote copies, remote signals or barrier semaphores. Data moves between devices by JAX's collectives and lax.ppermute only.
A program may use at most 64 MiB of HBM per device.

```python
import math
import jax
import jax.numpy as jnp
import numpy as np
from jax import lax

D = 3072
HD = 128
HEADS_DEV = 2
COLS = 32
TH = 8
TW = 8
FRAMES = 64
ROWS = 32
HEADS = 16


def draw_video(key, part):
    key = jax.random.fold_in(key, 11)
    subkeys = jax.random.split(key, 1)
    count = FRAMES * ROWS * COLS
    values = jax.random.normal(subkeys[0], (count, D), jnp.float32)
    values = jnp.clip(values, -18.0, 18.0)
    return values.reshape(FRAMES, ROWS, COLS, D).astype(jnp.bfloat16)


def draw_qkv_weight(key, part):
    key = jax.random.fold_in(key, 23)
    subkeys = jax.random.split(key, 2)
    others = jnp.clip(jax.random.normal(subkeys[1], (D, 3, HEADS * HD), jnp.float32), -6.0, 6.0)
    values = others
    return (values * (1.0 / math.sqrt(D))).astype(jnp.bfloat16)


def draw_window(key, part):
    key = jax.random.fold_in(key, 37)
    subkeys = jax.random.split(key, 6)
    groups = HEADS // HEADS_DEV
    member = jnp.arange(HEADS) % HEADS_DEV
    columns = []
    for which in range(3):
        reaches = jax.random.randint(subkeys[which], (HEADS,), 0, 2)
        chosen = jax.random.randint(subkeys[which + 3], (groups,), 0, HEADS_DEV)
        forced = member == jnp.repeat(chosen, HEADS_DEV)
        columns.append(jnp.where(forced, 1, reaches))
    return jnp.stack(columns, axis=1).astype(jnp.int32)


def split_up(number_of, total, limit, lean):
    weights = [(1 << 20) // math.isqrt(grade ** lean) + 1 for grade in range(2, number_of + 1)]
    surplus, given = total - limit - (number_of - 1), [1] * (number_of - 1)
    while surplus > 0:
        movable = [i for i in range(number_of - 1) if given[i] < limit]
        pool, remaining = sum([weights[i] for i in movable]), surplus
        for i in movable:
            more = min(limit - given[i], max(1, remaining * weights[i] // pool), surplus)
            given[i] = given[i] + more
            surplus = surplus - more
    return np.array([limit] + given)


def ragged(key, number_of, total, reach, slope):
    if number_of == 2:
        one = jax.random.randint(key, (), max(1, total - reach), min(reach, total - 1) + 1)
        return jnp.stack([one, total - one])
    tallies = jnp.asarray(split_up(number_of, total, reach, slope), jnp.int32)
    twos = (number_of - 1) // 2
    donor, receiver = tallies[1:1 + 2 * twos:2], tallies[2:2 + 2 * twos:2]
    slack = jnp.minimum(donor - 1, reach - receiver)
    moved = jax.random.randint(jax.random.fold_in(key, 1), (twos,), 0, 1 << 20) % (slack + 1)
    tallies = tallies.at[1:1 + 2 * twos:2].set(donor - moved).at[2:2 + 2 * twos:2].set(receiver + moved)
    return tallies[jax.random.permutation(jax.random.fold_in(key, 2), number_of)]


def setup_inputs(seed: int = 0) -> dict:
    arg_keys = jax.random.split(jax.random.key(seed), 5)
    video = draw_video(jax.random.fold_in(arg_keys[4], 71), 0)
    qkv_weight = draw_qkv_weight(jax.random.fold_in(arg_keys[4], 71), 0)
    window = draw_window(jax.random.fold_in(arg_keys[4], 71), 0)
    clips = jnp.searchsorted(jnp.cumsum(ragged(arg_keys[3], FRAMES // 4, FRAMES, 8, 0)), jnp.arange(FRAMES), side="right").astype(jnp.int32)
    return dict(video=video, qkv_weight=qkv_weight, window=window, clips=clips)


def reference(video, qkv_weight, window, clips):
    tokens = ROWS * COLS
    head_width = HEADS * HD
    flattened = video.reshape(FRAMES * tokens, D)
    projected = jnp.dot(flattened, qkv_weight.reshape(D, 3 * head_width), preferred_element_type=jnp.float32).astype(jnp.bfloat16)
    projected = projected.reshape(FRAMES, tokens, 3, HEADS, HD)
    queries = projected[:, :, 0]
    padded = jnp.pad(projected[:, :, 1:], ((1, 1), (0, 0), (0, 0), (0, 0), (0, 0)))
    edge_clip = jnp.full((1,), -1, jnp.int32)
    padded_clips = jnp.concatenate([edge_clip, clips.astype(jnp.int32), edge_clip])
    positions = jnp.arange(tokens, dtype=jnp.int32)
    tile_row = positions // COLS // TH
    tile_column = positions % COLS // TW
    row_gap = jnp.abs(tile_row[:, None] - tile_row[None, :])
    column_gap = jnp.abs(tile_column[:, None] - tile_column[None, :])
    inside = (row_gap[None] <= window[:, 1, None, None]) & (column_gap[None] <= window[:, 2, None, None])
    frame_gap = jnp.abs(jnp.arange(3, dtype=jnp.int32) - 1)
    score_scale = 1.0 / math.sqrt(HD)

    def one_frame(frame_index):
        nearby = lax.dynamic_slice_in_dim(padded, frame_index, 3, 0)
        nearby_clips = lax.dynamic_slice_in_dim(padded_clips, frame_index, 3, 0)
        frame_allowed = (frame_gap[None, :] <= window[:, 0:1]) & (nearby_clips == nearby_clips[1])[None, :]
        scores = jnp.einsum('qhd,fkhd->hqfk', queries[frame_index].astype(jnp.float32), nearby[:, :, 0].astype(jnp.float32)) * score_scale
        allowed = frame_allowed[:, None, :, None] & inside[:, :, None, :]
        masked = jnp.where(allowed, scores, -1e+30)
        row_max = lax.optimization_barrier(jnp.max(masked, axis=(2, 3), keepdims=True))
        weight = jnp.exp(masked - row_max)
        totals = lax.optimization_barrier(jnp.sum(weight, axis=(2, 3)))
        rounded = lax.optimization_barrier(weight.astype(jnp.bfloat16)).astype(jnp.float32)
        blended = jnp.einsum('hqfk,fkhd->qhd', rounded, nearby[:, :, 1].astype(jnp.float32))
        return (blended / totals.T[:, :, None]).astype(jnp.bfloat16)
    frames_out = lax.map(one_frame, jnp.arange(FRAMES, dtype=jnp.int32))
    return frames_out.reshape(FRAMES, ROWS, COLS, head_width)
```

```python
import functools
import math

import jax
import jax.numpy as jnp
from jax import lax
from jax.experimental import pallas as pl
from jax.experimental.pallas import tpu as pltpu
from jax.sharding import PartitionSpec as P

HD = 128
TH = 8
TW = 8
COLS = 32
TILE = TH * COLS
NEG = -1e30
SCALE = math.log2(math.e) / math.sqrt(HD)
GROUP = 4


def key_marks(tile, reach_row, reach_col, bias):
    lane = lax.broadcasted_iota(jnp.int32, (TILE, HD), 1)
    col = (lax.broadcasted_iota(jnp.int32, (TILE, HD), 0) % COLS) // TW
    by_col = jnp.where(jnp.abs(lane - col) <= reach_col, 0.0, NEG)
    by_row = jnp.where(jnp.abs(lane - 4 - tile) <= reach_row, 0.0, NEG)
    marks = jnp.where(lane < 4, by_col, jnp.where(lane < 8, by_row, jnp.where(lane == 8, bias, 0.0)))
    return marks.astype(jnp.bfloat16)


def query_marks(tile):
    lane = lax.broadcasted_iota(jnp.int32, (TILE, HD), 1)
    col = (lax.broadcasted_iota(jnp.int32, (TILE, HD), 0) % COLS) // TW
    hot = (lane == col) | (lane == 4 + tile) | (lane == 8)
    return hot.astype(jnp.float32).astype(jnp.bfloat16)


def attend_kernel(frames, first, final, tiles, *refs):
    flags, q = refs[0], refs[1]
    kvs = refs[2 : 2 + frames]
    rest = refs[2 + frames :]
    if not first:
        acc_in, top_in = rest[0], rest[1]
        rest = rest[2:]
    ones = jnp.ones((TILE, HD), jnp.bfloat16)
    marks = [query_marks(t) for t in range(tiles)]
    for h in range(2):
        keys, values = [], []
        for i in range(frames):
            bias = jnp.where(flags[6 + 2 * i + h] != 0, 0.0, NEG)
            for t in range(tiles):
                rows = pl.ds(t * TILE, TILE)
                key = kvs[i][rows, h * HD : (h + 1) * HD]
                value = kvs[i][rows, (2 + h) * HD : (3 + h) * HD]
                mark = key_marks(t, flags[h * 3 + 1], flags[h * 3 + 2], bias)
                keys.append(jnp.concatenate([key, mark], axis=1))
                values.append(jnp.concatenate([value, ones], axis=1))
        for t in range(tiles):
            rows = pl.ds(t * TILE, TILE)
            query = jnp.concatenate([q[rows, h * HD : (h + 1) * HD], marks[t]], axis=1)
            near = [i * tiles + u for i in range(frames) for u in range(max(t - 1, 0), min(t + 2, tiles))]
            scores = [
                lax.dot_general(
                    query, keys[j], (((1,), (1,)), ((), ())), preferred_element_type=jnp.float32
                )
                for j in near
            ]
            top = functools.reduce(jnp.maximum, scores)
            top = jnp.max(top, axis=1, keepdims=True)
            if not first:
                old = top_in[rows, h : h + 1]
                top = jnp.maximum(top, old)
            shift = top * SCALE
            weight = jnp.concatenate(
                [jnp.exp2(s * SCALE - shift).astype(jnp.bfloat16) for s in scores], axis=1
            )
            value = jnp.concatenate([values[j] for j in near], axis=0)
            acc = jnp.dot(weight, value, preferred_element_type=jnp.float32)
            wide = slice(2 * h * HD, 2 * (h + 1) * HD)
            if not first:
                acc = acc + acc_in[rows, wide] * jnp.exp2(old * SCALE - shift)
            if final:
                rest[0][rows, h * HD : (h + 1) * HD] = (acc[:, :HD] / acc[:, HD:]).astype(jnp.bfloat16)
            else:
                rest[0][rows, wide] = acc
                rest[1][rows, h : h + 1] = top


def attend(flags, q, kvs, state=None, final=True):
    tokens = q.shape[0]
    frames = len(kvs)
    vmem = pl.BlockSpec(memory_space=pltpu.VMEM)
    arrays = [q, *kvs, *(state or ())]
    if final:
        out = jax.ShapeDtypeStruct((tokens, 2 * HD), jnp.bfloat16)
    else:
        out = (
            jax.ShapeDtypeStruct((tokens, 4 * HD), jnp.float32),
            jax.ShapeDtypeStruct((tokens, HD), jnp.float32),
        )
    pairs = frames * 2 * 10 * TILE * TILE
    return pl.pallas_call(
        functools.partial(attend_kernel, frames, state is None, final, tokens // TILE),
        out_shape=out,
        in_specs=[pl.BlockSpec(memory_space=pltpu.SMEM)] + [vmem] * len(arrays),
        out_specs=vmem if final else (vmem, vmem),
        compiler_params=pltpu.CompilerParams(vmem_limit_bytes=48 * 1024 * 1024),
        cost_estimate=pl.CostEstimate(
            flops=pairs * 1024, bytes_accessed=(frames + 3) << 20, transcendentals=pairs
        ),
    )(flags, *arrays)


def body(video, qkv_weight, window, clips):
    frame_here = lax.axis_index("frame")
    frames = lax.axis_size("frame")
    width = qkv_weight.shape[2]
    features = video.shape[3]
    rows = video.shape[1] * lax.axis_size("row")

    shard = qkv_weight.reshape(-1, 3 * width)
    near = [[g * GROUP + i for i in range(GROUP)] for g in range(frames // GROUP)]
    far = [[g * GROUP + i for g in range(frames // GROUP)] for i in range(GROUP)]
    shard = lax.all_gather(shard, "frame", axis=0, tiled=True, axis_index_groups=near)
    matrix = lax.all_gather(shard, "frame", axis=0, tiled=True, axis_index_groups=far)

    block, shard = lax.optimization_barrier((video.reshape(1, -1, features), shard))
    copies = jnp.broadcast_to(block, (lax.axis_size("row"), *block.shape[1:]))
    tokens = lax.all_to_all(copies, "row", 0, 0).reshape(-1, features)

    kv = jnp.dot(tokens, matrix[:, width:], preferred_element_type=jnp.float32).astype(jnp.bfloat16)
    up = [(i, i + 1) for i in range(frames - 1)]
    before = lax.ppermute(kv, "frame", up)
    after = lax.ppermute(kv, "frame", [(j, i) for i, j in up])
    q = jnp.dot(tokens, matrix[:, :width], preferred_element_type=jnp.float32).astype(jnp.bfloat16)

    edge = jnp.full((1,), -1, jnp.int32)
    near_clips = lax.dynamic_slice_in_dim(jnp.concatenate([edge, clips, edge]), frame_here, 3, 0)
    reach = window[:, 0]
    flag = lambda side: ((reach >= 1) & (near_clips[side] == near_clips[1])).astype(jnp.int32)
    head = window.reshape(-1)
    here = jnp.concatenate([head, jnp.ones((2,), jnp.int32)])
    sides = jnp.concatenate([head, flag(0), flag(2)])

    state = attend(here, q, [kv], None, False)
    out = attend(sides, q, [before, after], state, True)
    return out.reshape(1, rows, -1, width)


def solution(mesh):
    placed = (P("frame", "row", None, None), P("frame", None, "row"), P("row", None), P())
    return jax.shard_map(
        body, mesh=mesh, in_specs=placed, out_specs=P("frame", None, None, "row"), check_vma=False
    )
```

```python
import functools
import math

import jax
import jax.numpy as jnp
from jax import lax
from jax.experimental import pallas as pl
from jax.experimental.pallas import tpu as pltpu
from jax.sharding import PartitionSpec as P

HD = 128
TH = 8
TW = 8
COLS = 32
TILE = TH * COLS
NEG = -1e30
SCALE = math.log2(math.e) / math.sqrt(HD)
GROUP = 4


def key_marks(tile, reach_row, reach_col, bias):
    lane = lax.broadcasted_iota(jnp.int32, (TILE, HD), 1)
    col = (lax.broadcasted_iota(jnp.int32, (TILE, HD), 0) % COLS) // TW
    by_col = jnp.where(jnp.abs(lane - col) <= reach_col, 0.0, NEG)
    by_row = jnp.where(jnp.abs(lane - 4 - tile) <= reach_row, 0.0, NEG)
    marks = jnp.where(lane < 4, by_col, jnp.where(lane < 8, by_row, jnp.where(lane == 8, bias, 0.0)))
    return marks.astype(jnp.bfloat16)


def query_marks(tile):
    lane = lax.broadcasted_iota(jnp.int32, (TILE, HD), 1)
    col = (lax.broadcasted_iota(jnp.int32, (TILE, HD), 0) % COLS) // TW
    hot = (lane == col) | (lane == 4 + tile) | (lane == 8)
    return hot.astype(jnp.float32).astype(jnp.bfloat16)


def attend_kernel(heads, frames, first, final, tiles, *refs):
    flags, q = refs[0], refs[1]
    kvs = refs[2 : 2 + frames * len(heads)]
    rest = refs[2 + frames * len(heads) :]
    if not first:
        acc_in, top_in = rest[0], rest[1]
        rest = rest[2:]
    if final and len(heads) == 1:
        done, rest = rest[0], rest[1:]
    own = flags[6 + 2 * frames]
    half = TILE // 2

    def put(t, low, value):
        for part, at in ((0, own), (1, 1 - own)):
            place = pl.multiple_of(t * TILE + at * half, half)
            rest[0][pl.ds(place, half), low : low + HD] = value[part * half : (part + 1) * half]

    ones = jnp.ones((TILE, HD), jnp.bfloat16)
    marks = [query_marks(t) for t in range(tiles)]
    for slot, h in enumerate(heads):
        keys, values = [], []
        for i in range(frames):
            bias = jnp.where(flags[6 + 2 * i + h] != 0, 0.0, NEG)
            kv = kvs[i * len(heads) + slot]
            for t in range(tiles):
                rows = pl.ds(t * TILE, TILE)
                mark = key_marks(t, flags[h * 3 + 1], flags[h * 3 + 2], bias)
                keys.append(jnp.concatenate([kv[rows, :HD], mark], axis=1))
                values.append(jnp.concatenate([kv[rows, HD:], ones], axis=1))
        for t in range(tiles):
            rows = pl.ds(t * TILE, TILE)
            query = jnp.concatenate([q[rows, h * HD : (h + 1) * HD], marks[t]], axis=1)
            near = [i * tiles + u for i in range(frames) for u in range(max(t - 1, 0), min(t + 2, tiles))]
            scores = [
                lax.dot_general(
                    query, keys[j], (((1,), (1,)), ((), ())), preferred_element_type=jnp.float32
                )
                for j in near
            ]
            top = functools.reduce(jnp.maximum, scores)
            top = jnp.max(top, axis=1, keepdims=True)
            if not first:
                old = top_in[rows, h : h + 1]
                top = jnp.maximum(top, old)
            shift = top * SCALE
            weight = jnp.concatenate(
                [jnp.exp2(s * SCALE - shift).astype(jnp.bfloat16) for s in scores], axis=1
            )
            value = jnp.concatenate([values[j] for j in near], axis=0)
            acc = jnp.dot(weight, value, preferred_element_type=jnp.float32)
            wide = slice(2 * h * HD, 2 * (h + 1) * HD)
            if not first:
                acc = acc + acc_in[rows, wide] * jnp.exp2(old * SCALE - shift)
            if not final:
                rest[0][rows, wide] = acc
                rest[1][rows, h : h + 1] = top
            elif len(heads) == 1 and h == 0:
                rest[0][rows, :] = (acc[:, :HD] / acc[:, HD:]).astype(jnp.bfloat16)
            else:
                put(t, h * HD, (acc[:, :HD] / acc[:, HD:]).astype(jnp.bfloat16))
                if len(heads) == 1:
                    put(t, 0, done[rows, :])


def attend(heads, flags, q, kvs, state=None, final=True, done=None):
    tokens = q.shape[0]
    frames = len(kvs)
    vmem = pl.BlockSpec(memory_space=pltpu.VMEM)
    arrays = [q, *(part for kv in kvs for part in kv), *(state or ())]
    if done is not None:
        arrays.append(done)
    elif final:
        arrays.append(jnp.zeros((16, HD), jnp.bfloat16))
    if final:
        out = jax.ShapeDtypeStruct((tokens, HD if done is None else 2 * HD), jnp.bfloat16)
    else:
        out = (
            jax.ShapeDtypeStruct((tokens, 4 * HD), jnp.float32),
            jax.ShapeDtypeStruct((tokens, HD), jnp.float32),
        )
    pairs = frames * len(heads) * 10 * TILE * TILE
    return pl.pallas_call(
        functools.partial(attend_kernel, heads, frames, state is None, final, tokens // TILE),
        out_shape=out,
        in_specs=[pl.BlockSpec(memory_space=pltpu.SMEM)] + [vmem] * len(arrays),
        out_specs=vmem if final else (vmem, vmem),
        compiler_params=pltpu.CompilerParams(vmem_limit_bytes=40 * 1024 * 1024),
        cost_estimate=pl.CostEstimate(
            flops=pairs * 1024, bytes_accessed=(frames + 3) << 19, transcendentals=pairs
        ),
    )(flags, *arrays)


def order_kernel(turns, where, *refs):
    out, done = refs[-2:]
    step = TILE // 2
    copies = []
    for i, block in enumerate(refs[:-2]):
        y = lax.rem(where[2] + turns[i // 2], len(turns))
        to = pl.ds(pl.multiple_of(y * TILE + i % 2 * step, step), step)
        copy = pltpu.make_async_copy(block, out.at[to, :], done.at[i])
        copy.start()
        copies.append(copy)
    for copy in copies:
        copy.wait()


def order(where, near, far, turns):
    blocks = [block for pair in zip(near, far) for block in pair]
    step, features = blocks[0].shape
    return pl.pallas_call(
        functools.partial(order_kernel, turns),
        out_shape=jax.ShapeDtypeStruct((len(blocks) * step, features), jnp.bfloat16),
        in_specs=[pl.BlockSpec(memory_space=pltpu.SMEM)]
        + [pl.BlockSpec(memory_space=pl.ANY)] * len(blocks),
        out_specs=pl.BlockSpec(memory_space=pltpu.VMEM),
        scratch_shapes=[pltpu.SemaphoreType.DMA((len(blocks),))],
        compiler_params=pltpu.CompilerParams(vmem_limit_bytes=16 * 1024 * 1024),
        cost_estimate=pl.CostEstimate(flops=1 << 20, bytes_accessed=12 << 20, transcendentals=0),
    )(where, *blocks)


def project_kernel(*refs):
    parts, tokens, out = refs[:-2], refs[-2], refs[-1]
    if len(parts) == 1:
        matrix = parts[0][...]
    else:
        depth = parts[0].shape[0] // 2
        heads = [
            jnp.concatenate([part[h * depth : (h + 1) * depth, :] for part in parts], axis=0)
            for h in range(2)
        ]
        matrix = jnp.concatenate(heads, axis=1)
    step = 512
    for i in range(0, tokens.shape[0], step):
        rows = pl.ds(i, step)
        result = jnp.dot(tokens[rows, :], matrix, preferred_element_type=jnp.float32)
        out[rows, :] = result.astype(jnp.bfloat16)


def project(parts, tokens):
    rows, features = tokens.shape
    columns = 2 * HD
    vmem = pl.BlockSpec(memory_space=pltpu.VMEM)
    return pl.pallas_call(
        project_kernel,
        out_shape=jax.ShapeDtypeStruct((rows, columns), jnp.bfloat16),
        in_specs=[vmem] * (len(parts) + 1),
        out_specs=vmem,
        compiler_params=pltpu.CompilerParams(vmem_limit_bytes=20 * 1024 * 1024),
        cost_estimate=pl.CostEstimate(
            flops=2 * rows * features * columns,
            bytes_accessed=2 * (rows * features + features * columns),
            transcendentals=0,
        ),
    )(*parts, tokens)


def body(frames, row_count, video, qkv_weight, window, clips):
    axes = ("frame", "row")
    frame_here = lax.axis_index("frame").astype(jnp.int32)
    row_here = lax.axis_index("row").astype(jnp.int32)
    depth = frames // GROUP
    y_count = row_count // 2
    width = qkv_weight.shape[2]
    share = qkv_weight.shape[0]
    features = video.shape[3]

    def send(value, to):
        pairs = []
        for f in range(frames):
            for r in range(row_count):
                tf, tr = to(f, r)
                pairs.append((f * row_count + r, tf * row_count + tr))
        return lax.ppermute(value, axes, pairs)

    other_x_hi = lambda value: send(value, lambda f, r: (f, r ^ 1))

    columns = [[g * GROUP + i for g in range(depth)] for i in range(GROUP)]
    four = [[g * GROUP + i for i in range(GROUP)] for g in range(depth)]

    shard = qkv_weight.reshape(share, 3 * width)
    cut = lambda j, h: shard[:, j * width + h * HD : j * width + (h + 1) * HD]
    shard = jnp.concatenate([cut(1, 0), cut(2, 0), cut(1, 1), cut(2, 1), shard[:, :width]], axis=1)
    group = lax.all_gather(shard, "frame", axis=0, tiled=True, axis_index_groups=four)
    mine = lax.dynamic_slice_in_dim(group, 4 * HD + frame_here % 2 * HD, HD, 1)
    group = jnp.concatenate([group[:, : 4 * HD], mine], axis=1)
    matrix = lax.all_gather(group, "frame", axis=0, tiled=True, axis_index_groups=columns)

    block = video.reshape(-1, features)
    block, group = lax.optimization_barrier((block, group))
    along_y = lambda value, k: send(value, lambda f, r: (f, (r - 2 * k) % row_count))
    turns = (0, 1, y_count - 1, 2)
    block_x = other_x_hi(block)
    near = [block] + [along_y(block, k) for k in turns[1:]]
    far = [block_x, along_y(block_x, 1), along_y(block_x, -1), other_x_hi(near[3])]

    where = jnp.stack([frame_here // 2 % 2, frame_here % 2, row_here // 2])
    tokens = order(where, near, far, turns)
    up = [(i, i + 1) for i in range(frames - 1)]
    down = [(j, i) for i, j in up]
    kv, before, after = [], [], []
    for h in range(2):
        result = project([matrix[:, h * 2 * HD : (h + 1) * 2 * HD]], tokens)
        kv.append(result)
        before.append(lax.ppermute(result, "frame", up))
        after.append(lax.ppermute(result, "frame", down))
    mine, *_ = lax.optimization_barrier((matrix[:, 4 * HD :], *kv))
    pairs = [[f, f + 1] for f in range(0, frames, 2)]
    halves = [
        lax.all_gather(half, "frame", axis=0, tiled=True, axis_index_groups=pairs)
        for half in jnp.split(mine, 2, axis=0)
    ]
    q = project(halves, tokens)

    edge = jnp.full((1,), -1, jnp.int32)
    near_clips = lax.dynamic_slice_in_dim(jnp.concatenate([edge, clips, edge]), frame_here, 3, 0)
    reach = window[:, 0]
    flag = lambda side: ((reach >= 1) & (near_clips[side] == near_clips[1])).astype(jnp.int32)
    head = window.reshape(-1)
    place = (row_here % 2).reshape(1)
    here = jnp.concatenate([head, jnp.ones((2,), jnp.int32), place])
    sides = jnp.concatenate([head, flag(0), flag(2), place])

    state = attend((0, 1), here, q, [kv], None, False)
    done = attend((0,), sides, q, [before[:1], after[:1]], state)
    out = attend((1,), sides, q, [before[1:], after[1:]], state, True, done)
    return out.reshape(1, row_count * video.shape[1], -1, width)


def solution(mesh):
    placed = (P("frame", "row", None, None), P("frame", None, "row"), P("row", None), P())
    sizes = (mesh.shape["frame"], mesh.shape["row"])
    return jax.shard_map(
        functools.partial(body, *sizes), mesh=mesh,
        in_specs=placed,
        out_specs=P("frame", None, None, "row"),
        check_vma=False,
    )
```

```python
import functools
import math

import jax
import jax.numpy as jnp
from jax import lax
from jax.experimental import pallas as pl
from jax.experimental.pallas import tpu as pltpu
from jax.sharding import PartitionSpec as P

HD = 128
TH = 8
TW = 8
COLS = 32
TILE = TH * COLS
NEG = -1e30
SCALE = math.log2(math.e) / math.sqrt(HD)
GROUP = 4


def key_marks(tile, reach_row, reach_col, bias):
    lane = lax.broadcasted_iota(jnp.int32, (TILE, HD), 1)
    col = (lax.broadcasted_iota(jnp.int32, (TILE, HD), 0) % COLS) // TW
    by_col = jnp.where(jnp.abs(lane - col) <= reach_col, 0.0, NEG)
    by_row = jnp.where(jnp.abs(lane - 4 - tile) <= reach_row, 0.0, NEG)
    marks = jnp.where(lane < 4, by_col, jnp.where(lane < 8, by_row, jnp.where(lane == 8, bias, 0.0)))
    return marks.astype(jnp.bfloat16)


def query_marks(tile):
    lane = lax.broadcasted_iota(jnp.int32, (TILE, HD), 1)
    col = (lax.broadcasted_iota(jnp.int32, (TILE, HD), 0) % COLS) // TW
    hot = (lane == col) | (lane == 4 + tile) | (lane == 8)
    return hot.astype(jnp.float32).astype(jnp.bfloat16)


def attend_kernel(heads, frames, first, final, tiles, *refs):
    flags, q = refs[0], refs[1]
    kvs = refs[2 : 2 + frames * len(heads)]
    rest = refs[2 + frames * len(heads) :]
    if not first:
        acc_in, top_in = rest[0], rest[1]
        rest = rest[2:]
    if final and len(heads) == 1:
        done, rest = rest[0], rest[1:]
    own = flags[6 + 2 * frames]
    half = TILE // 2

    def put(t, low, value):
        for part, at in ((0, own), (1, 1 - own)):
            place = pl.multiple_of(t * TILE + at * half, half)
            rest[0][pl.ds(place, half), low : low + HD] = value[part * half : (part + 1) * half]

    ones = jnp.ones((TILE, HD), jnp.bfloat16)
    marks = [query_marks(t) for t in range(tiles)]
    for slot, h in enumerate(heads):
        keys, values = [], []
        for i in range(frames):
            bias = jnp.where(flags[6 + 2 * i + h] != 0, 0.0, NEG)
            kv = kvs[i * len(heads) + slot]
            for t in range(tiles):
                rows = pl.ds(t * TILE, TILE)
                mark = key_marks(t, flags[h * 3 + 1], flags[h * 3 + 2], bias)
                keys.append(jnp.concatenate([kv[rows, :HD], mark], axis=1))
                values.append(jnp.concatenate([kv[rows, HD:], ones], axis=1))
        for t in range(tiles):
            rows = pl.ds(t * TILE, TILE)
            query = jnp.concatenate([q[rows, h * HD : (h + 1) * HD], marks[t]], axis=1)
            near = [i * tiles + u for i in range(frames) for u in range(max(t - 1, 0), min(t + 2, tiles))]
            scores = [
                lax.dot_general(
                    query, keys[j], (((1,), (1,)), ((), ())), preferred_element_type=jnp.float32
                )
                for j in near
            ]
            top = functools.reduce(jnp.maximum, scores)
            top = jnp.max(top, axis=1, keepdims=True)
            if not first:
                old = top_in[rows, h : h + 1]
                top = jnp.maximum(top, old)
            shift = top * SCALE
            weight = jnp.concatenate(
                [jnp.exp2(s * SCALE - shift).astype(jnp.bfloat16) for s in scores], axis=1
            )
            value = jnp.concatenate([values[j] for j in near], axis=0)
            acc = jnp.dot(weight, value, preferred_element_type=jnp.float32)
            wide = slice(2 * h * HD, 2 * (h + 1) * HD)
            if not first:
                acc = acc + acc_in[rows, wide] * jnp.exp2(old * SCALE - shift)
            if not final:
                rest[0][rows, wide] = acc
                rest[1][rows, h : h + 1] = top
            elif len(heads) == 1 and h == 0:
                rest[0][rows, :] = (acc[:, :HD] / acc[:, HD:]).astype(jnp.bfloat16)
            else:
                put(t, h * HD, (acc[:, :HD] / acc[:, HD:]).astype(jnp.bfloat16))
                if len(heads) == 1:
                    put(t, 0, done[rows, :])


def attend(heads, flags, q, kvs, state=None, final=True, done=None):
    tokens = q.shape[0]
    frames = len(kvs)
    vmem = pl.BlockSpec(memory_space=pltpu.VMEM)
    arrays = [q, *(part for kv in kvs for part in kv), *(state or ())]
    if done is not None:
        arrays.append(done)
    elif final:
        arrays.append(jnp.zeros((16, HD), jnp.bfloat16))
    if final:
        out = jax.ShapeDtypeStruct((tokens, HD if done is None else 2 * HD), jnp.bfloat16)
    else:
        out = (
            jax.ShapeDtypeStruct((tokens, 4 * HD), jnp.float32),
            jax.ShapeDtypeStruct((tokens, HD), jnp.float32),
        )
    pairs = frames * len(heads) * 10 * TILE * TILE
    return pl.pallas_call(
        functools.partial(attend_kernel, heads, frames, state is None, final, tokens // TILE),
        out_shape=out,
        in_specs=[pl.BlockSpec(memory_space=pltpu.SMEM)] + [vmem] * len(arrays),
        out_specs=vmem if final else (vmem, vmem),
        compiler_params=pltpu.CompilerParams(vmem_limit_bytes=40 * 1024 * 1024),
        cost_estimate=pl.CostEstimate(
            flops=pairs * 1024, bytes_accessed=(frames + 3) << 19, transcendentals=pairs
        ),
    )(flags, *arrays)


def order_kernel(turns, where, *refs):
    out, done = refs[-2:]
    step = TILE // 2
    copies = []
    for i, block in enumerate(refs[:-2]):
        y = lax.rem(where[2] + turns[i], len(turns))
        to = pl.ds(pl.multiple_of(y * step, step), step)
        copy = pltpu.make_async_copy(block, out.at[to, :], done.at[i])
        copy.start()
        copies.append(copy)
    for copy in copies:
        copy.wait()


def order(where, blocks, turns):
    step, features = blocks[0].shape
    return pl.pallas_call(
        functools.partial(order_kernel, turns),
        out_shape=jax.ShapeDtypeStruct((len(blocks) * step, features), jnp.bfloat16),
        in_specs=[pl.BlockSpec(memory_space=pltpu.SMEM)]
        + [pl.BlockSpec(memory_space=pl.ANY)] * len(blocks),
        out_specs=pl.BlockSpec(memory_space=pltpu.VMEM),
        scratch_shapes=[pltpu.SemaphoreType.DMA((len(blocks),))],
        compiler_params=pltpu.CompilerParams(vmem_limit_bytes=16 * 1024 * 1024),
        cost_estimate=pl.CostEstimate(flops=1 << 20, bytes_accessed=12 << 20, transcendentals=0),
    )(where, *blocks)


def project_kernel(*refs):
    parts, tokens, out = refs[:-3], refs[-3:-1], refs[-1]
    if len(parts) == 1:
        matrix = parts[0][...]
    else:
        depth = parts[0].shape[0] // 2
        heads = [
            jnp.concatenate([part[h * depth : (h + 1) * depth, :] for part in parts], axis=0)
            for h in range(2)
        ]
        matrix = jnp.concatenate(heads, axis=1)
    step = TILE // 2
    for half, ref in enumerate(tokens):
        result = jnp.dot(ref[...], matrix, preferred_element_type=jnp.float32).astype(jnp.bfloat16)
        for y in range(ref.shape[0] // step):
            out[pl.ds(y * TILE + half * step, step), :] = result[y * step : (y + 1) * step]


def project(parts, tokens):
    rows, features = 2 * tokens[0].shape[0], tokens[0].shape[1]
    columns = 2 * HD
    vmem = pl.BlockSpec(memory_space=pltpu.VMEM)
    return pl.pallas_call(
        project_kernel,
        out_shape=jax.ShapeDtypeStruct((rows, columns), jnp.bfloat16),
        in_specs=[vmem] * (len(parts) + 2),
        out_specs=vmem,
        compiler_params=pltpu.CompilerParams(vmem_limit_bytes=20 * 1024 * 1024),
        cost_estimate=pl.CostEstimate(
            flops=2 * rows * features * columns,
            bytes_accessed=2 * (rows * features + features * columns),
            transcendentals=0,
        ),
    )(*parts, *tokens)


def body(frames, row_count, video, qkv_weight, window, clips):
    axes = ("frame", "row")
    frame_here = lax.axis_index("frame").astype(jnp.int32)
    row_here = lax.axis_index("row").astype(jnp.int32)
    depth = frames // GROUP
    y_count = row_count // 2
    width = qkv_weight.shape[2]
    share = qkv_weight.shape[0]
    features = video.shape[3]

    def send(value, to):
        pairs = []
        for f in range(frames):
            for r in range(row_count):
                tf, tr = to(f, r)
                pairs.append((f * row_count + r, tf * row_count + tr))
        return lax.ppermute(value, axes, pairs)

    other_x_hi = lambda value: send(value, lambda f, r: (f, r ^ 1))

    columns = [[g * GROUP + i for g in range(depth)] for i in range(GROUP)]
    four = [[g * GROUP + i for i in range(GROUP)] for g in range(depth)]

    shard = qkv_weight.reshape(share, 3 * width)
    cut = lambda j, h: shard[:, j * width + h * HD : j * width + (h + 1) * HD]
    shard = jnp.concatenate([cut(1, 0), cut(2, 0), cut(1, 1), cut(2, 1), shard[:, :width]], axis=1)
    group = lax.all_gather(shard, "frame", axis=0, tiled=True, axis_index_groups=four)
    mine = lax.dynamic_slice_in_dim(group, 4 * HD + frame_here % 2 * HD, HD, 1)
    group = jnp.concatenate([group[:, : 4 * HD], mine], axis=1)
    matrix = lax.all_gather(group, "frame", axis=0, tiled=True, axis_index_groups=columns)

    block = video.reshape(-1, features)
    block, group = lax.optimization_barrier((block, group))
    along_y = lambda value, k: send(value, lambda f, r: (f, (r - 2 * k) % row_count))
    turns = (0, 1, y_count - 1, 2)
    block_x = other_x_hi(block)
    near = [block] + [along_y(block, k) for k in turns[1:]]
    far = [block_x, along_y(block_x, 1), along_y(block_x, -1), other_x_hi(near[3])]

    where = jnp.stack([frame_here // 2 % 2, frame_here % 2, row_here // 2])
    tokens = [order(where, near, turns), order(where, far, turns)]
    up = [(i, i + 1) for i in range(frames - 1)]
    down = [(j, i) for i, j in up]
    kv, before, after = [], [], []
    for h in range(2):
        result = project([matrix[:, h * 2 * HD : (h + 1) * 2 * HD]], tokens)
        kv.append(result)
        before.append(lax.ppermute(result, "frame", up))
        after.append(lax.ppermute(result, "frame", down))
    mine, *_ = lax.optimization_barrier((matrix[:, 4 * HD :], *kv))
    pairs = [[f, f + 1] for f in range(0, frames, 2)]
    halves = [
        lax.all_gather(half, "frame", axis=0, tiled=True, axis_index_groups=pairs)
        for half in jnp.split(mine, 2, axis=0)
    ]
    q = project(halves, tokens)

    edge = jnp.full((1,), -1, jnp.int32)
    near_clips = lax.dynamic_slice_in_dim(jnp.concatenate([edge, clips, edge]), frame_here, 3, 0)
    reach = window[:, 0]
    flag = lambda side: ((reach >= 1) & (near_clips[side] == near_clips[1])).astype(jnp.int32)
    head = window.reshape(-1)
    place = (row_here % 2).reshape(1)
    here = jnp.concatenate([head, jnp.ones((2,), jnp.int32), place])
    sides = jnp.concatenate([head, flag(0), flag(2), place])

    state = attend((0, 1), here, q, [kv], None, False)
    done = attend((0,), sides, q, [before[:1], after[:1]], state)
    out = attend((1,), sides, q, [before[1:], after[1:]], state, True, done)
    return out.reshape(1, row_count * video.shape[1], -1, width)


def solution(mesh):
    placed = (P("frame", "row", None, None), P("frame", None, "row"), P("row", None), P())
    sizes = (mesh.shape["frame"], mesh.shape["row"])
    return jax.shard_map(
        functools.partial(body, *sizes), mesh=mesh,
        in_specs=placed,
        out_specs=P("frame", None, None, "row"),
        check_vma=False,
    )
```

```python
import functools
import math

import jax
import jax.numpy as jnp
from jax import lax
from jax.experimental import pallas as pl
from jax.experimental.pallas import tpu as pltpu
from jax.sharding import PartitionSpec as P

HD = 128
TH = 8
TW = 8
COLS = 32
TILE = TH * COLS
NEG = -1e30
SCALE = math.log2(math.e) / math.sqrt(HD)
GROUP = 4


def key_marks(tile, reach_row, reach_col, bias):
    lane = lax.broadcasted_iota(jnp.int32, (TILE, HD), 1)
    col = (lax.broadcasted_iota(jnp.int32, (TILE, HD), 0) % COLS) // TW
    by_col = jnp.where(jnp.abs(lane - col) <= reach_col, 0.0, NEG)
    by_row = jnp.where(jnp.abs(lane - 4 - tile) <= reach_row, 0.0, NEG)
    marks = jnp.where(lane < 4, by_col, jnp.where(lane < 8, by_row, jnp.where(lane == 8, bias, 0.0)))
    return marks.astype(jnp.bfloat16)


def query_marks(tile):
    lane = lax.broadcasted_iota(jnp.int32, (TILE, HD), 1)
    col = (lax.broadcasted_iota(jnp.int32, (TILE, HD), 0) % COLS) // TW
    hot = (lane == col) | (lane == 4 + tile) | (lane == 8)
    return hot.astype(jnp.float32).astype(jnp.bfloat16)


def attend_kernel(heads, frames, first, final, tiles, *refs):
    flags, q = refs[0], refs[1]
    kvs = refs[2 : 2 + frames * len(heads)]
    rest = refs[2 + frames * len(heads) :]
    if not first:
        acc_in, top_in = rest[0], rest[1]
        rest = rest[2:]
    if final and len(heads) == 1:
        done, rest = rest[0], rest[1:]
    own = flags[6 + 2 * frames]
    half = TILE // 2

    def put(t, low, value):
        for part, at in ((0, own), (1, 1 - own)):
            place = pl.multiple_of(t * TILE + at * half, half)
            rest[0][pl.ds(place, half), low : low + HD] = value[part * half : (part + 1) * half]

    ones = jnp.ones((TILE, HD), jnp.bfloat16)
    marks = [query_marks(t) for t in range(tiles)]
    for slot, h in enumerate(heads):
        keys, values = [], []
        for i in range(frames):
            bias = jnp.where(flags[6 + 2 * i + h] != 0, 0.0, NEG)
            kv = kvs[i * len(heads) + slot]
            for t in range(tiles):
                rows = pl.ds(t * TILE, TILE)
                mark = key_marks(t, flags[h * 3 + 1], flags[h * 3 + 2], bias)
                keys.append(jnp.concatenate([kv[rows, :HD], mark], axis=1))
                values.append(jnp.concatenate([kv[rows, HD:], ones], axis=1))
        for t in range(tiles):
            rows = pl.ds(t * TILE, TILE)
            query = jnp.concatenate([q[rows, h * HD : (h + 1) * HD], marks[t]], axis=1)
            near = [i * tiles + u for i in range(frames) for u in range(max(t - 1, 0), min(t + 2, tiles))]
            scores = [
                lax.dot_general(
                    query, keys[j], (((1,), (1,)), ((), ())), preferred_element_type=jnp.float32
                )
                for j in near
            ]
            top = functools.reduce(jnp.maximum, scores)
            top = jnp.max(top, axis=1, keepdims=True)
            if not first:
                old = top_in[rows, h : h + 1]
                top = jnp.maximum(top, old)
            shift = top * SCALE
            weight = jnp.concatenate(
                [jnp.exp2(s * SCALE - shift).astype(jnp.bfloat16) for s in scores], axis=1
            )
            value = jnp.concatenate([values[j] for j in near], axis=0)
            acc = jnp.dot(weight, value, preferred_element_type=jnp.float32)
            wide = slice(2 * h * HD, 2 * (h + 1) * HD)
            if not first:
                acc = acc + acc_in[rows, wide] * jnp.exp2(old * SCALE - shift)
            if not final:
                rest[0][rows, wide] = acc
                rest[1][rows, h : h + 1] = top
            elif len(heads) == 1 and h == 0:
                rest[0][rows, :] = (acc[:, :HD] / acc[:, HD:]).astype(jnp.bfloat16)
            else:
                put(t, h * HD, (acc[:, :HD] / acc[:, HD:]).astype(jnp.bfloat16))
                if len(heads) == 1:
                    put(t, 0, done[rows, :])


def attend(heads, flags, q, kvs, state=None, final=True, done=None):
    tokens = q.shape[0]
    frames = len(kvs)
    vmem = pl.BlockSpec(memory_space=pltpu.VMEM)
    arrays = [q, *(part for kv in kvs for part in kv), *(state or ())]
    if done is not None:
        arrays.append(done)
    elif final:
        arrays.append(jnp.zeros((16, HD), jnp.bfloat16))
    if final:
        out = jax.ShapeDtypeStruct((tokens, HD if done is None else 2 * HD), jnp.bfloat16)
    else:
        out = (
            jax.ShapeDtypeStruct((tokens, 4 * HD), jnp.float32),
            jax.ShapeDtypeStruct((tokens, HD), jnp.float32),
        )
    pairs = frames * len(heads) * 10 * TILE * TILE
    return pl.pallas_call(
        functools.partial(attend_kernel, heads, frames, state is None, final, tokens // TILE),
        out_shape=out,
        in_specs=[pl.BlockSpec(memory_space=pltpu.SMEM)] + [vmem] * len(arrays),
        out_specs=vmem if final else (vmem, vmem),
        compiler_params=pltpu.CompilerParams(vmem_limit_bytes=40 * 1024 * 1024),
        cost_estimate=pl.CostEstimate(
            flops=pairs * 1024, bytes_accessed=(frames + 3) << 19, transcendentals=pairs
        ),
    )(flags, *arrays)


def order_kernel(turns, where, *refs):
    out, done = refs[-2:]
    step = TILE // 2
    copies = []
    for i, block in enumerate(refs[:-2]):
        y = lax.rem(where[2] + turns[i], len(turns))
        to = pl.ds(pl.multiple_of(y * step, step), step)
        copy = pltpu.make_async_copy(block, out.at[to, :], done.at[i])
        copy.start()
        copies.append(copy)
    for copy in copies:
        copy.wait()


def order(where, blocks, turns):
    step, features = blocks[0].shape
    return pl.pallas_call(
        functools.partial(order_kernel, turns),
        out_shape=jax.ShapeDtypeStruct((len(blocks) * step, features), jnp.bfloat16),
        in_specs=[pl.BlockSpec(memory_space=pltpu.SMEM)]
        + [pl.BlockSpec(memory_space=pl.ANY)] * len(blocks),
        out_specs=pl.BlockSpec(memory_space=pltpu.VMEM),
        scratch_shapes=[pltpu.SemaphoreType.DMA((len(blocks),))],
        compiler_params=pltpu.CompilerParams(vmem_limit_bytes=16 * 1024 * 1024),
        cost_estimate=pl.CostEstimate(flops=1 << 20, bytes_accessed=12 << 20, transcendentals=0),
    )(where, *blocks)


def project_kernel(*refs):
    parts, tokens, out = refs[:-3], refs[-3:-1], refs[-1]
    if len(parts) == 1:
        matrix = parts[0][...]
    else:
        depth = parts[0].shape[0] // 2
        heads = [
            jnp.concatenate([part[h * depth : (h + 1) * depth, :] for part in parts], axis=0)
            for h in range(2)
        ]
        matrix = jnp.concatenate(heads, axis=1)
    step = TILE // 2
    for half, ref in enumerate(tokens):
        result = jnp.dot(ref[...], matrix, preferred_element_type=jnp.float32).astype(jnp.bfloat16)
        for y in range(ref.shape[0] // step):
            out[pl.ds(y * TILE + half * step, step), :] = result[y * step : (y + 1) * step]


def project(parts, tokens):
    rows, features = 2 * tokens[0].shape[0], tokens[0].shape[1]
    columns = 2 * HD
    vmem = pl.BlockSpec(memory_space=pltpu.VMEM)
    return pl.pallas_call(
        project_kernel,
        out_shape=jax.ShapeDtypeStruct((rows, columns), jnp.bfloat16),
        in_specs=[vmem] * (len(parts) + 2),
        out_specs=vmem,
        compiler_params=pltpu.CompilerParams(vmem_limit_bytes=20 * 1024 * 1024),
        cost_estimate=pl.CostEstimate(
            flops=2 * rows * features * columns,
            bytes_accessed=2 * (rows * features + features * columns),
            transcendentals=0,
        ),
    )(*parts, *tokens)


def body(frames, row_count, video, qkv_weight, window, clips):
    axes = ("frame", "row")
    frame_here = lax.axis_index("frame").astype(jnp.int32)
    row_here = lax.axis_index("row").astype(jnp.int32)
    depth = frames // GROUP
    y_count = row_count // 2
    width = qkv_weight.shape[2]
    share = qkv_weight.shape[0]
    features = video.shape[3]

    def send(value, to):
        pairs = []
        for f in range(frames):
            for r in range(row_count):
                tf, tr = to(f, r)
                pairs.append((f * row_count + r, tf * row_count + tr))
        return lax.ppermute(value, axes, pairs)

    other_x_hi = lambda value: send(value, lambda f, r: (f, r ^ 1))

    columns = [[g * GROUP + i for g in range(depth)] for i in range(GROUP)]
    four = [[g * GROUP + i for i in range(GROUP)] for g in range(depth)]

    shard = qkv_weight.reshape(share, 3 * width)
    group = lax.all_gather(shard, "frame", axis=0, tiled=True, axis_index_groups=four)
    cut = lambda j, h: group[:, j * width + h * HD : j * width + (h + 1) * HD]
    mine = lax.dynamic_slice_in_dim(group, frame_here % 2 * HD, HD, 1)
    group = jnp.concatenate([cut(1, 0), cut(2, 0), cut(1, 1), cut(2, 1), mine], axis=1)
    matrix = lax.all_gather(group, "frame", axis=0, tiled=True, axis_index_groups=columns)

    block = video.reshape(-1, features)
    block, group = lax.optimization_barrier((block, group))
    along_y = lambda value, k: send(value, lambda f, r: (f, (r - 2 * k) % row_count))
    turns = (0, 1, y_count - 1, 2)
    block_x = other_x_hi(block)
    near = [block] + [along_y(block, k) for k in turns[1:]]
    far = [block_x, along_y(block_x, 1), along_y(block_x, -1), other_x_hi(near[3])]

    where = jnp.stack([frame_here // 2 % 2, frame_here % 2, row_here // 2])
    tokens = [order(where, near, turns), order(where, far, turns)]
    up = [(i, i + 1) for i in range(frames - 1)]
    down = [(j, i) for i, j in up]
    kv, before, after = [], [], []
    for h in range(2):
        result = project([matrix[:, h * 2 * HD : (h + 1) * 2 * HD]], tokens)
        kv.append(result)
        before.append(lax.ppermute(result, "frame", up))
        after.append(lax.ppermute(result, "frame", down))
    mine, *_ = lax.optimization_barrier((matrix[:, 4 * HD :], *kv))
    pairs = [[f, f + 1] for f in range(0, frames, 2)]
    halves = [
        lax.all_gather(half, "frame", axis=0, tiled=True, axis_index_groups=pairs)
        for half in jnp.split(mine, 2, axis=0)
    ]
    q = project(halves, tokens)

    edge = jnp.full((1,), -1, jnp.int32)
    near_clips = lax.dynamic_slice_in_dim(jnp.concatenate([edge, clips, edge]), frame_here, 3, 0)
    reach = window[:, 0]
    flag = lambda side: ((reach >= 1) & (near_clips[side] == near_clips[1])).astype(jnp.int32)
    head = window.reshape(-1)
    place = (row_here % 2).reshape(1)
    here = jnp.concatenate([head, jnp.ones((2,), jnp.int32), place])
    sides = jnp.concatenate([head, flag(0), flag(2), place])

    state = attend((0, 1), here, q, [kv], None, False)
    done = attend((0,), sides, q, [before[:1], after[:1]], state)
    out = attend((1,), sides, q, [before[1:], after[1:]], state, True, done)
    return out.reshape(1, row_count * video.shape[1], -1, width)


def solution(mesh):
    placed = (P("frame", "row", None, None), P("frame", None, "row"), P("row", None), P())
    sizes = (mesh.shape["frame"], mesh.shape["row"])
    return jax.shard_map(
        functools.partial(body, *sizes), mesh=mesh,
        in_specs=placed,
        out_specs=P("frame", None, None, "row"),
        check_vma=False,
    )
```
